32 devices in a mesh: row: 4 (over x, core), col: 8 (over z, y).
Axes of the slice: x: 2, y: 2, z: 4, core: 2. Of those that a mesh axis runs over, the one named last changes fastest.
Arguments:
- inv_diag: float32 [2, 2048, 2048], P(None, 'row', 'col'), may hold values from -1 to 2, as said below
- coupling: float32 [2048, 2048], P('row', 'col'), may hold values from -0.125 to 0.125
- top_rhs: float32 [2, 2048, 1024], P(None, 'row', 'col'), may hold values from -6 to 6
- panel: float32 [2, 4096, 2048], P(None, 'row', 'col'), may hold values from -0.125 to 0.125
- rhs: float32 [4096, 1024], P('row', 'col'), may hold values from -6 to 6
Outputs:
- solved: float32 [2, 2048, 1024], P(None, 'row', 'col')
- trailing: float32 [4096, 1024], P('row', 'col')
The draws below stay inside these ranges and needn't reach their ends.
Inputs may be any that keep to these rules, and one draw needn't show every extreme that they name: `inv_diag`: each of the two blocks is lower triangular with its diagonal in 1 to 2.
All inputs are finite; a program needn't handle non-finite values.
Results may differ from the reference program's by a relative error of at most 0.000073.
Values sent between devices are 32-bit elements; how exact they have to be, the bound alone decides.
No kernel may reach another device: no remote copies, remote signals or barrier semaphores. Data moves between devices by JAX's collectives and lax.ppermute only.
A program may use at most 64 MiB of HBM per device.

```python
import jax
import jax.numpy as jnp
from jax import lax

NB = 2048
M = 4096
TIME = 1024


def draw_inv_diag(key, part):
    shape = (2, NB, NB)
    rowpos = lax.broadcasted_iota(jnp.int32, shape, 1)
    colpos = lax.broadcasted_iota(jnp.int32, shape, 2)
    key_off, key_diag = jax.random.split(key)
    below = jnp.clip(jax.random.normal(key_off, shape, jnp.float32) / NB ** 0.5, -0.5, 0.5)
    diagonal = jax.random.uniform(key_diag, shape, jnp.float32, 1.0, 2.0)
    value = jnp.where(rowpos > colpos, below, jnp.where(rowpos == colpos, diagonal, 0.0))
    value = jnp.where((rowpos == 1) & (colpos == 0), -1.0, value)
    value = jnp.where((rowpos == 0) & (colpos == 0), 2.0, value)
    return value.astype(jnp.float32)


def levels(key, extent, cuts, low, high):
    gain = 1.0
    for axis_at, shards_of in cuts:
        steps = jax.random.uniform(jax.random.fold_in(jax.random.fold_in(key, 6), axis_at), (shards_of,), jnp.float32, low / len(cuts), high / len(cuts))
        gain = gain * jnp.repeat(jnp.exp(steps), extent[axis_at] // shards_of).reshape((-1,) + (1,) * (len(extent) - 1 - axis_at))
    return gain


def noise(stream_key, extent, width, reach, pieces=(), held_as=jnp.bfloat16):
    array = jax.random.normal(stream_key, extent, jnp.float32) * width
    if len(pieces) > 0:
        array = levels(stream_key, extent, pieces, -0.22, 0.18) * array
    return jnp.clip(array, min=-reach, max=reach).astype(held_as)


def setup_inputs(seed: int = 0) -> dict:
    keys = jax.random.split(jax.random.key(seed), 6)
    return {
        "inv_diag": draw_inv_diag(jax.random.fold_in(keys[5], 71), 0),
        "coupling": noise(keys[1], (NB, NB), NB ** -0.5, 0.125, ((0, 4), (1, 8)), jnp.float32),
        "top_rhs": noise(keys[2], (2, NB, TIME), 1.0, 6.0, ((1, 4), (2, 8)), jnp.float32),
        "panel": noise(keys[3], (2, M, NB), NB ** -0.5, 0.125, ((1, 4), (2, 8)), jnp.float32),
        "rhs": noise(keys[4], (M, TIME), 1.0, 6.0, ((0, 4), (1, 8)), jnp.float32),
    }


def product(left, right):
    return jnp.dot(left, right, precision=lax.Precision.HIGHEST, preferred_element_type=jnp.float32)


def reference(inv_diag, coupling, top_rhs, panel, rhs):
    first = product(inv_diag[0], top_rhs[0])
    reduced = top_rhs[1] - product(coupling, first)
    second = product(inv_diag[1], reduced)
    solved = jnp.stack([first, second])
    trailing = rhs - (product(panel[0], first) + product(panel[1], second))
    return solved, trailing
```

```python
import functools

import jax
import jax.numpy as jnp
from jax import lax
from jax.experimental import pallas as pl
from jax.experimental.pallas import tpu as pltpu
from jax.sharding import PartitionSpec as P

F32 = jnp.float32
BF16 = jnp.bfloat16
VMEM_LIMIT = 48 * 1024 * 1024


def split(value):
    high = value.astype(BF16)
    return high, (value - high.astype(F32)).astype(BF16)


def dot(left, right):
    return jnp.dot(left, right, preferred_element_type=F32)


def product(left, right):
    left_high, left_low = split(left)
    right_high, right_low = split(right)
    return dot(left_high, right_high) + (dot(left_high, right_low) + dot(left_low, right_high))


def stage_kernel(parts, where_ref, *refs):
    matrices, vector_ref, out_ref = refs[:parts], refs[parts], refs[parts + 1]
    blocks, shards, rows, depth = matrices[0].shape
    pieces = []
    for b in range(shards):
        start = pl.multiple_of(where_ref[b] * depth, depth)
        pieces.append(split(vector_ref[pl.ds(start, depth), :]))
    for part in range(parts):
        for k in range(blocks):
            total = None
            for b in range(shards):
                high, low = split(matrices[part][k, b])
                v_high, v_low = pieces[b]
                term = dot(high, v_high) + (dot(high, v_low) + dot(low, v_high))
                total = term if total is None else total + term
            out_ref[k, part * rows:(part + 1) * rows, :] = total


def stage(matrices, vector, where):
    parts = len(matrices)
    blocks, shards, rows, depth = matrices[0].shape
    width = vector.shape[1]
    return pl.pallas_call(
        functools.partial(stage_kernel, parts),
        out_shape=jax.ShapeDtypeStruct((blocks, parts * rows, width), F32),
        in_specs=[pl.BlockSpec(memory_space=pltpu.SMEM)]
        + [pl.BlockSpec(memory_space=pltpu.VMEM)] * (parts + 1),
        out_specs=pl.BlockSpec(memory_space=pltpu.VMEM),
        compiler_params=pltpu.CompilerParams(vmem_limit_bytes=VMEM_LIMIT),
        cost_estimate=pl.CostEstimate(
            flops=6 * blocks * shards * parts * rows * depth * width,
            bytes_accessed=4 * parts * blocks * shards * rows * depth + 4 * blocks * parts * rows * width,
            transcendentals=0,
        ),
    )(where, *matrices, vector)


def panel_kernel(shards, where_ref, *refs):
    panels, solved_refs, out_ref = refs[:shards], refs[shards:shards + 2], refs[shards + 2]
    depth = panels[0].shape[2]
    blocks = out_ref.shape[0]
    total = [None] * blocks
    for half in range(2):
        for b in range(shards):
            high, low = split(panels[b][half])
            start = pl.multiple_of(where_ref[b] * depth, depth)
            for k in range(blocks):
                v_high, v_low = split(solved_refs[half][k, pl.ds(start, depth), :])
                term = dot(high, v_high) + (dot(high, v_low) + dot(low, v_high))
                if half == 0 and b == 0:
                    out_ref[k] = term
                else:
                    out_ref[k] += term


def panel_product(panels, first, second, where):
    shards = len(panels)
    blocks, _, width = first.shape
    _, rows, depth = panels[0].shape
    return pl.pallas_call(
        functools.partial(panel_kernel, shards),
        out_shape=jax.ShapeDtypeStruct((blocks, rows, width), F32),
        in_specs=[pl.BlockSpec(memory_space=pltpu.SMEM)]
        + [pl.BlockSpec(memory_space=pltpu.VMEM)] * (shards + 2),
        out_specs=pl.BlockSpec(memory_space=pltpu.VMEM),
        compiler_params=pltpu.CompilerParams(vmem_limit_bytes=VMEM_LIMIT),
        cost_estimate=pl.CostEstimate(
            flops=12 * blocks * shards * rows * depth * width,
            bytes_accessed=8 * shards * rows * depth + 4 * blocks * rows * width,
            transcendentals=0,
        ),
    )(where, *panels, first, second)


def bits(count):
    found = []
    bit = count // 2
    while bit >= 1:
        found.append(bit)
        bit //= 2
    return found


def after(value, *earlier):
    return lax.optimization_barrier((value, *earlier))[0]


class Grid:
    def __init__(self, mesh):
        self.rows = mesh.shape["row"]
        self.cols = mesh.shape["col"]
        self.shards = self.cols // self.rows

    def move(self, value, target):
        pairs = []
        for r in range(self.rows):
            for a in range(self.rows):
                for b in range(self.shards):
                    to = target(r, a, b)
                    if to is not None:
                        pairs.append((
                            r * self.cols + a * self.shards + b,
                            to[0] * self.cols + to[1] * self.shards + to[2],
                        ))
        return lax.ppermute(value, ("row", "col"), pairs)

    def swap(self, value):
        return self.move(value, lambda r, a, b: (a, r, b))

    def row_bit(self, value, bit):
        return self.move(value, lambda r, a, b: (r ^ bit, a, b))

    def b_bit(self, value, bit):
        return self.move(value, lambda r, a, b: (r, a, b ^ bit))

    def gather_b(self, value, axis):
        for bit in reversed(bits(self.shards)):
            value = jnp.concatenate([value, self.b_bit(value, bit)], axis)
        return value

    def gather_row_far(self, value, axis):
        for bit in bits(self.rows)[:-1]:
            value = jnp.concatenate([value, self.row_bit(value, bit)], axis)
        return value

    def gather_row_near(self, value, axis):
        return jnp.concatenate([value, self.row_bit(value, 1)], axis)

    def row_order(self):
        order = [0]
        for bit in bits(self.rows):
            order = order + [o ^ bit for o in order]
        return order

    def gather_matrix(self, value):
        half = value.shape[0] // 2
        upper = value[:half][None, None]
        lower = value[half:][None, None]
        upper = self.gather_row_far(self.gather_b(upper, 1), 0)
        lower = self.gather_b(self.gather_row_far(lower, 0), 1)
        return self.gather_row_near(upper, 0), self.gather_row_near(lower, 0)

    def line_sum(self, block, a, two_way):
        n = self.rows
        right, left = None, None
        for step in range(1, n):
            send = block(jnp.clip(n - step + a, 0, n - 1))
            if right is not None:
                send = send + right
            right = self.move(
                send, lambda r, p, b: (r, p + 1, b) if p <= min(step - 1, n - 2) else None
            )
            if two_way:
                send = block(jnp.clip(step - 1 - (n - 1 - a), 0, n - 1))
                if left is not None:
                    send = send + left
                left = self.move(
                    send, lambda r, p, b: (r, p - 1, b) if p >= max(n - step, 1) else None
                )
        total = block(a) + right
        return total + left if two_way else total


def solution(mesh):
    grid = Grid(mesh)
    order = grid.row_order()
    place = [order.index(o) for o in range(grid.rows)]

    def body(inv_diag, coupling, top_rhs, panel, rhs):
        r = lax.axis_index("row")
        c = lax.axis_index("col")
        a, b = c // grid.shards, c % grid.shards
        places = jnp.array(place, jnp.int32)
        where = jnp.stack([b ^ o for o in range(grid.shards)]).astype(jnp.int32)

        def picker(blocks):
            def pick(j):
                return lax.dynamic_index_in_dim(blocks, places[j ^ r], 0, keepdims=False)

            return pick

        record_one = grid.swap(top_rhs[0])
        inverse_one = grid.gather_matrix(inv_diag[0])
        coupled = grid.gather_matrix(after(coupling, inverse_one[0]))
        record_two = grid.swap(after(top_rhs[1], record_one))
        inverse_two = grid.gather_matrix(after(inv_diag[1], coupled[0]))
        panels = [panel]
        gathered = after(panel, inverse_two[0])
        for o in range(1, grid.shards):
            panels.append(grid.b_bit(gathered, o))

        first = grid.line_sum(picker(stage(inverse_one, record_one, where)), a, False)
        term = grid.line_sum(picker(stage(coupled, first, where)), a, True)
        reduced = record_two - term
        first_all = grid.gather_row_near(grid.gather_row_far(first[None], 0), 0)
        solved_one = grid.swap(first)
        second = grid.line_sum(picker(stage(inverse_two, reduced, where)), a, False)
        second_all = grid.gather_row_near(grid.gather_row_far(second[None], 0), 0)
        solved_two = grid.swap(after(second, second_all))
        update = grid.line_sum(picker(panel_product(panels, first_all, second_all, where)), a, True)
        return jnp.stack([solved_one, solved_two]), rhs - update

    in_specs = (
        P(None, "row", "col"),
        P("row", "col"),
        P(None, "row", "col"),
        P(None, "row", "col"),
        P("row", "col"),
    )
    out_specs = (P(None, "row", "col"), P("row", "col"))
    return jax.shard_map(body, mesh=mesh, in_specs=in_specs, out_specs=out_specs, check_vma=False)
```

```python
import functools

import jax
import jax.numpy as jnp
from jax import lax
from jax.experimental import pallas as pl
from jax.experimental.pallas import tpu as pltpu
from jax.sharding import PartitionSpec as P

F32 = jnp.float32
BF16 = jnp.bfloat16
VMEM_LIMIT = 32 * 1024 * 1024
SMEM = pl.BlockSpec(memory_space=pltpu.SMEM)
HBM = pl.BlockSpec(memory_space=pltpu.HBM)


def split(value):
    high = value.astype(BF16)
    return high, (value - high.astype(F32)).astype(BF16)


def dot(left, right):
    return jnp.dot(left, right, preferred_element_type=F32)


def product(left, right):
    return dot(left[0], right[0]) + (dot(left[0], right[1]) + dot(left[1], right[0]))


def shape(dtype, *dims):
    return jax.ShapeDtypeStruct(dims, dtype)


def call(kernel, outs, scratch, flops, where, *operands):
    moved = sum(v.size * v.dtype.itemsize for v in (*operands, *outs))
    return pl.pallas_call(
        kernel,
        out_shape=outs,
        in_specs=[SMEM] + [HBM] * len(operands),
        out_specs=[HBM] * len(outs),
        scratch_shapes=scratch,
        compiler_params=pltpu.CompilerParams(vmem_limit_bytes=VMEM_LIMIT),
        cost_estimate=pl.CostEstimate(flops=flops, bytes_accessed=moved, transcendentals=0),
    )(where, *operands)


def start(source, target, sem):
    copy = pltpu.make_async_copy(source, target, sem)
    copy.start()
    return copy


def stage_kernel(places, shards, blocks, record, where_ref, *refs):
    count = len(places)
    pieces, given = refs[:count], refs[count:-blocks - 7]
    vector_out, outs = refs[-blocks - 7], refs[-blocks - 6:-6]
    matrix_ref, given_ref, vector_ref, product_ref, sems, given_sems = refs[-6:]
    arrivals = [start(ref, given_ref.at[i], given_sems.at[i]) for i, ref in enumerate(given)] if not record else []
    core = where_ref[shards + 1]
    if record:
        width = given[0].shape[1]
        for i, side in enumerate((core, 1 - core)):
            lanes = pl.ds(pl.multiple_of(side * width, width), width)
            arrivals.append(start(given[i], vector_ref.at[:, lanes], given_sems.at[i]))
        arrivals += [start(ref, given_ref.at[i], given_sems.at[2 + i]) for i, ref in enumerate(given[2:])]
    copies = [start(pieces[i], matrix_ref.at[place], sems.at[i]) for i, place in enumerate(places)]
    offset = where_ref[shards]
    for copy in arrivals:
        copy.wait()
    if not record:
        vector_ref[...] = given_ref[0] + given_ref[1]
    elif len(given) > 2:
        vector_ref[...] = vector_ref[...] - (given_ref[0] + given_ref[1])
    leaving = [start(vector_ref, vector_out, given_sems.at[0])]
    product_ref[blocks // 2] = jnp.zeros_like(product_ref[blocks // 2])
    depth = vector_ref.shape[0] // shards
    parts = [
        split(vector_ref[pl.ds(pl.multiple_of(where_ref[o] * depth, depth), depth), :]) for o in range(shards)
    ]
    for k in range(blocks // 2):
        for i, place in enumerate(places):
            if place[0] == k:
                copies[i].wait()
        sums = [product(split(matrix_ref[k, o]), parts[o]) for o in range(shards)]
        product_ref[k] = sum(sums[1:], sums[0])
    for d in range(blocks):
        k = jnp.bitwise_xor(offset, d) // 2
        if d == 0:
            k = jnp.where(lax.rem(offset, 2) == 1, blocks // 2, k)
        leaving.append(start(product_ref.at[k], outs[d], sems.at[d]))
    for copy in leaving:
        copy.wait()


def stage(blocks, where, matrix, *given, record):
    shards = len(matrix) * 2 // blocks
    rows, depth = matrix[0, 0].shape
    width = given[0].shape[1] * (2 if record else 1)
    outs = [shape(F32, shards * depth, width)] + [shape(F32, rows, width)] * blocks
    scratch = [
        pltpu.VMEM((blocks // 2, shards, rows, depth), F32),
        pltpu.VMEM((2, shards * depth, width), F32),
        pltpu.VMEM((shards * depth, width), F32),
        pltpu.VMEM((blocks // 2 + 1, rows, width), F32),
        pltpu.SemaphoreType.DMA((max(len(matrix), blocks),)),
        pltpu.SemaphoreType.DMA((4,)),
    ]
    kernel = functools.partial(stage_kernel, list(matrix), shards, blocks, record)
    flops = 3 * blocks * rows * shards * depth * width
    found = call(kernel, outs, scratch, flops, where, *matrix.values(), *given)
    return found[0], list(found[1:])


def panel_kernel(shards, blocks, parts, where_ref, *refs):
    panels, pairs = refs[:shards], refs[shards:shards + blocks // 2 * parts]
    earlier = refs[shards + len(pairs):-blocks - 9]
    outs = refs[-blocks - 9:-9]
    panel_ref, pair_ref, p_high, p_low, v_high, v_low, total_ref, sems, out_sems = refs[-9:]
    width, depth = total_ref.shape[2], panel_ref.shape[2]
    copies = [start(ref, pair_ref.at[i], sems.at[i]) for i, ref in enumerate(pairs)]
    copies += [start(ref, panel_ref.at[o], sems.at[len(pairs) + o]) for o, ref in enumerate(panels)]
    loads = [start(ref, total_ref.at[d], out_sems.at[d]) for d, ref in enumerate(earlier)]
    for copy in copies[:len(pairs)]:
        copy.wait()
    for k in range(blocks // 2):
        for o in range(shards):
            rows = pl.ds(pl.multiple_of(where_ref[blocks + o] * depth, depth), depth)
            value = pair_ref[k * parts, rows, :]
            for i in range(1, parts):
                value = value + pair_ref[k * parts + i, rows, :]
            high, low = split(value)
            for side in range(2):
                lanes = slice(side * width, (side + 1) * width)
                v_high[2 * k + side, o * depth:(o + 1) * depth, :] = high[:, lanes]
                v_low[2 * k + side, o * depth:(o + 1) * depth, :] = low[:, lanes]
    for o, copy in enumerate(copies[len(pairs):]):
        copy.wait()
        p_high[:, o * depth:(o + 1) * depth], p_low[:, o * depth:(o + 1) * depth] = split(panel_ref[o])
    leaving = []
    for d in reversed(range(blocks)):
        k = where_ref[d]
        high, low = v_high[k], v_low[k]
        both = dot(p_high[...], jnp.concatenate([high, low], 1))
        total = both[:, :width] + (both[:, width:] + dot(p_low[...], high))
        if earlier:
            loads[d].wait()
            total = total_ref[d] + total
        total_ref[d] = total
        leaving.append(start(total_ref.at[d], outs[d], out_sems.at[d]))
    for copy in leaving:
        copy.wait()


def panel_product(where, panel, pairs, earlier):
    shards, blocks, parts = len(panel), len(pairs) * 2, len(pairs[0])
    rows, depth = panel[0].shape
    width = pairs[0][0].shape[1]
    given = [part for pair in pairs for part in pair]
    outs = [shape(F32, rows, width // 2)] * blocks
    scratch = [
        pltpu.VMEM((shards, rows, depth), F32),
        pltpu.VMEM((len(given), shards * depth, width), F32),
        pltpu.VMEM((rows, shards * depth), BF16),
        pltpu.VMEM((rows, shards * depth), BF16),
        pltpu.VMEM((blocks, shards * depth, width // 2), BF16),
        pltpu.VMEM((blocks, shards * depth, width // 2), BF16),
        pltpu.VMEM((blocks, rows, width // 2), F32),
        pltpu.SemaphoreType.DMA((len(given) + shards,)),
        pltpu.SemaphoreType.DMA((blocks,)),
    ]
    kernel = functools.partial(panel_kernel, shards, blocks, parts)
    flops = 3 * blocks * rows * shards * depth * width
    return list(call(kernel, outs, scratch, flops, where, *panel, *given, *earlier))


def after(value, *earlier):
    return lax.optimization_barrier((value, *earlier))[0]


def together(*values):
    return list(lax.optimization_barrier(values))


class Grid:
    def __init__(self, mesh):
        self.rows = mesh.shape["row"]
        self.cols = mesh.shape["col"]
        self.shards = self.cols // self.rows

    def move(self, value, target):
        pairs = []
        for r in range(self.rows):
            for a in range(self.rows):
                for b in range(self.shards):
                    to = target(r, a, b)
                    if to is not None:
                        pairs.append((
                            r * self.cols + a * self.shards + b,
                            to[0] * self.cols + to[1] * self.shards + to[2],
                        ))
        return lax.ppermute(value, ("row", "col"), pairs)

    def swap(self, value):
        return self.move(value, lambda r, a, b: (a, r, b))

    def row_bit(self, value, bit):
        return self.move(value, lambda r, a, b: (r ^ bit, a, b))

    def gather_b(self, value):
        return {(0, o): self.b_bit(value, o) if o else value for o in range(self.shards)}

    def b_bit(self, value, bit):
        return self.move(value, lambda r, a, b: (r, a, b ^ bit))

    def gather_row(self, pieces):
        found = dict(pieces)
        for k in range(2, self.rows, 2):
            for (_, o), piece in pieces.items():
                found[k // 2, o] = self.row_bit(piece, k)
        return found

    def send(self, blocks, two_way):
        total = blocks[0]
        got = []
        for d in reversed(range(1, self.rows)):
            got.append(self.move(
                blocks[d],
                lambda r, a, b: (r, a ^ d, b)
                if (r ^ a ^ d) % 2 == 0 and (two_way or (a ^ d) > a) else None,
            ))
        for block in got:
            total = total + block
        return total

    def both(self, total):
        return total, self.row_bit(total, 1)

    def pair_send(self, blocks, last):
        sums = {d: blocks[d] for d in range(0, self.rows, 2)}
        for d in reversed(range(3, self.rows, 2)):
            sums[d - 1] = sums[d - 1] + self.move(blocks[d], lambda r, a, b: (r, a ^ 1, b))
        got = [self.move(after(blocks[1], *last), lambda r, a, b: (r, a ^ 1, b))]
        for d in reversed(range(2, self.rows, 2)):
            got.append(self.move(sums[d], lambda r, a, b: (r, a ^ d, b)))
        return [blocks[0], *got]


def solution(mesh):
    grid = Grid(mesh)
    rows, shards = grid.rows, grid.shards

    def body(inv_diag, coupling, top_rhs, panel, rhs):
        r = lax.axis_index("row")
        c = lax.axis_index("col")
        a, b = c // shards, c % shards
        where = jnp.stack([b ^ o for o in range(shards)] + [a ^ r, r % 2]).astype(jnp.int32)
        planes = [a ^ d for d in range(rows)]
        slots = [(j ^ r) // 2 * 2 + j % 2 for j in planes] + [b ^ o for o in range(shards)]
        slots = jnp.stack(slots).astype(jnp.int32)
        run = functools.partial(stage, rows, where)
        width = top_rhs.shape[2]

        record_one = grid.swap(top_rhs[0])
        inverse_one = grid.gather_b(inv_diag[0])
        far = {(k // 2, 0): grid.row_bit(inv_diag[0], k) for k in range(2, rows, 2)}
        early = [record_one, *inverse_one.values(), *far.values()]
        for k in range(2, rows, 2):
            for o in range(1, shards):
                far[k // 2, o] = grid.move(inv_diag[0], lambda r, a, b: (r ^ k, a, b ^ o))
        inverse_one |= far
        held = after(coupling, *early)
        coupled = grid.gather_b(held)
        coupled |= {(k // 2, 0): grid.row_bit(held, k) for k in range(2, rows, 2)}
        record_two = grid.swap(after(top_rhs[1], *early))
        first_in = grid.both(record_one)
        first_in = together(*first_in, record_two)[:2]
        _, blocks = run(inverse_one, *first_in, record=True)

        for k in range(2, rows, 2):
            for o in range(1, shards):
                coupled[k // 2, o] = grid.row_bit(after(coupled[0, o], blocks[0]), k)
        panel_one = grid.gather_b(after(panel[0], *inverse_one.values()))
        held = after(inv_diag[1], *coupled.values())
        sums = list(grid.both(grid.send(blocks, False)))
        sums[0] = after(sums[0], *panel_one.values())
        first, blocks = run(coupled, *sums, record=False)
        inverse_two = grid.gather_row(grid.gather_b(held))
        panel_two = grid.gather_b(after(panel[1], *panel_one.values()))
        sums = list(grid.both(grid.send(blocks, True)))
        sums[0] = after(sums[0], *panel_two.values())
        firsts = [[grid.row_bit(first, k) if k else first] for k in range(0, rows, 2)]
        _, blocks = run(inverse_two, *grid.both(record_two), *sums, record=True)
        earlier = panel_product(slots, list(panel_one.values()), firsts, [])
        total = grid.send(blocks, False)
        total = after(total, *earlier)
        seconds = [list(grid.both(grid.row_bit(total, k) if k else total)) for k in range(0, rows, 2)]
        second = seconds[0][0] + seconds[0][1]
        solved = grid.swap(lax.dynamic_slice_in_dim(jnp.stack([first, second]), r % 2 * width, width, 2))
        blocks = panel_product(slots, list(panel_two.values()), seconds, earlier)
        arrived = grid.pair_send(blocks, [solved])
        return solved, rhs - sum(arrived[1:], arrived[0])

    in_specs = (
        P(None, "row", "col"),
        P("row", "col"),
        P(None, "row", "col"),
        P(None, "row", "col"),
        P("row", "col"),
    )
    out_specs = (P(None, "row", "col"), P("row", "col"))
    return jax.shard_map(body, mesh=mesh, in_specs=in_specs, out_specs=out_specs, check_vma=False)
```

```python
import functools

import jax
import jax.numpy as jnp
from jax import lax
from jax.experimental import pallas as pl
from jax.experimental.pallas import tpu as pltpu
from jax.sharding import PartitionSpec as P

F32 = jnp.float32
BF16 = jnp.bfloat16
VMEM_LIMIT = 32 * 1024 * 1024
SMEM = pl.BlockSpec(memory_space=pltpu.SMEM)
HBM = pl.BlockSpec(memory_space=pltpu.HBM)


def split(value):
    high = value.astype(BF16)
    return high, (value - high.astype(F32)).astype(BF16)


def dot(left, right):
    return jnp.dot(left, right, preferred_element_type=F32)


def product(left, right):
    return dot(left[0], right[0]) + (dot(left[0], right[1]) + dot(left[1], right[0]))


def shape(dtype, *dims):
    return jax.ShapeDtypeStruct(dims, dtype)


def call(kernel, outs, scratch, flops, where, *operands):
    moved = sum(v.size * v.dtype.itemsize for v in (*operands, *outs))
    return pl.pallas_call(
        kernel,
        out_shape=outs,
        in_specs=[SMEM] + [HBM] * len(operands),
        out_specs=[HBM] * len(outs),
        scratch_shapes=scratch,
        compiler_params=pltpu.CompilerParams(vmem_limit_bytes=VMEM_LIMIT),
        cost_estimate=pl.CostEstimate(flops=flops, bytes_accessed=moved, transcendentals=0),
    )(where, *operands)


def start(source, target, sem):
    copy = pltpu.make_async_copy(source, target, sem)
    copy.start()
    return copy


def stage_kernel(places, shards, blocks, record, where_ref, *refs):
    count = len(places)
    pieces, given = refs[:count], refs[count:-blocks - 7]
    vector_out, outs = refs[-blocks - 7], refs[-blocks - 6:-6]
    matrix_ref, given_ref, vector_ref, product_ref, sems, given_sems = refs[-6:]
    arrivals = [start(ref, given_ref.at[i], given_sems.at[i]) for i, ref in enumerate(given)] if not record else []
    core = where_ref[shards + 1]
    if record:
        width = given[0].shape[1]
        for i, side in enumerate((core, 1 - core)):
            lanes = pl.ds(pl.multiple_of(side * width, width), width)
            arrivals.append(start(given[i], vector_ref.at[:, lanes], given_sems.at[i]))
        arrivals += [start(ref, given_ref.at[i], given_sems.at[2 + i]) for i, ref in enumerate(given[2:])]
    copies = []
    for i, (k, o, row) in enumerate(places):
        part = matrix_ref.at[k, o, pl.ds(row, pieces[i].shape[0])]
        copies.append(start(pieces[i], part, sems.at[i]))
    offset = where_ref[shards]
    for copy in arrivals:
        copy.wait()
    if not record:
        vector_ref[...] = given_ref[0] + given_ref[1]
    elif len(given) > 2:
        vector_ref[...] = vector_ref[...] - (given_ref[0] + given_ref[1])
    leaving = [start(vector_ref, vector_out, given_sems.at[0])]
    product_ref[blocks // 2] = jnp.zeros_like(product_ref[blocks // 2])
    depth = vector_ref.shape[0] // shards
    parts = [
        split(vector_ref[pl.ds(pl.multiple_of(where_ref[o] * depth, depth), depth), :]) for o in range(shards)
    ]
    for k in range(blocks // 2):
        for i, place in enumerate(places):
            if place[0] == k:
                copies[i].wait()
        sums = [product(split(matrix_ref[k, o]), parts[o]) for o in range(shards)]
        product_ref[k] = sum(sums[1:], sums[0])
    for d in range(blocks):
        k = jnp.bitwise_xor(offset, d) // 2
        if d == 0:
            k = jnp.where(lax.rem(offset, 2) == 1, blocks // 2, k)
        leaving.append(start(product_ref.at[k], outs[d], sems.at[d]))
    for copy in leaving:
        copy.wait()


def stage(blocks, where, matrix, *given, record):
    rows, depth = matrix[0, 0, 0].shape
    shards = 1 + max(o for _, o, _ in matrix)
    width = given[0].shape[1] * (2 if record else 1)
    outs = [shape(F32, shards * depth, width)] + [shape(F32, rows, width)] * blocks
    scratch = [
        pltpu.VMEM((blocks // 2, shards, rows, depth), F32),
        pltpu.VMEM((2, shards * depth, width), F32),
        pltpu.VMEM((shards * depth, width), F32),
        pltpu.VMEM((blocks // 2 + 1, rows, width), F32),
        pltpu.SemaphoreType.DMA((max(len(matrix), blocks),)),
        pltpu.SemaphoreType.DMA((4,)),
    ]
    kernel = functools.partial(stage_kernel, list(matrix), shards, blocks, record)
    flops = 3 * blocks * rows * shards * depth * width
    found = call(kernel, outs, scratch, flops, where, *matrix.values(), *given)
    return found[0], list(found[1:])


def panel_kernel(shards, blocks, parts, wanted, where_ref, *refs):
    panels, pairs = refs[:shards], refs[shards:shards + blocks // 2 * parts]
    earlier = refs[shards + len(pairs):-len(wanted) - 9]
    outs = refs[-len(wanted) - 9:-9]
    panel_ref, pair_ref, p_high, p_low, v_high, v_low, total_ref, sems, out_sems = refs[-9:]
    width, depth = total_ref.shape[2], panel_ref.shape[2]
    copies = [start(ref, pair_ref.at[i], sems.at[i]) for i, ref in enumerate(pairs)]
    copies += [start(ref, panel_ref.at[o], sems.at[len(pairs) + o]) for o, ref in enumerate(panels)]
    loads = [start(ref, total_ref.at[d], out_sems.at[d]) for d, ref in enumerate(earlier)]
    for copy in copies[:len(pairs)]:
        copy.wait()
    for k in range(blocks // 2):
        for o in range(shards):
            rows = pl.ds(pl.multiple_of(where_ref[blocks + o] * depth, depth), depth)
            value = pair_ref[k * parts, rows, :]
            for i in range(1, parts):
                value = value + pair_ref[k * parts + i, rows, :]
            high, low = split(value)
            for side in range(2):
                lanes = slice(side * width, (side + 1) * width)
                v_high[2 * k + side, o * depth:(o + 1) * depth, :] = high[:, lanes]
                v_low[2 * k + side, o * depth:(o + 1) * depth, :] = low[:, lanes]
    for o, copy in enumerate(copies[len(pairs):]):
        copy.wait()
        p_high[:, o * depth:(o + 1) * depth], p_low[:, o * depth:(o + 1) * depth] = split(panel_ref[o])
    leaving = []
    for i, d in enumerate(wanted):
        k = where_ref[d]
        high, low = v_high[k], v_low[k]
        both = dot(p_high[...], jnp.concatenate([high, low], 1))
        total = both[:, :width] + (both[:, width:] + dot(p_low[...], high))
        if earlier:
            loads[i].wait()
            total = total_ref[i] + total
        total_ref[i] = total
        leaving.append(start(total_ref.at[i], outs[i], out_sems.at[i]))
    for copy in leaving:
        copy.wait()


def panel_product(where, panel, pairs, earlier, wanted):
    shards, blocks, parts = len(panel), len(pairs) * 2, len(pairs[0])
    rows, depth = panel[0].shape
    width = pairs[0][0].shape[1]
    given = [part for pair in pairs for part in pair]
    outs = [shape(F32, rows, width // 2)] * len(wanted)
    scratch = [
        pltpu.VMEM((shards, rows, depth), F32),
        pltpu.VMEM((len(given), shards * depth, width), F32),
        pltpu.VMEM((rows, shards * depth), BF16),
        pltpu.VMEM((rows, shards * depth), BF16),
        pltpu.VMEM((blocks, shards * depth, width // 2), BF16),
        pltpu.VMEM((blocks, shards * depth, width // 2), BF16),
        pltpu.VMEM((len(wanted), rows, width // 2), F32),
        pltpu.SemaphoreType.DMA((len(given) + shards,)),
        pltpu.SemaphoreType.DMA((len(wanted),)),
    ]
    kernel = functools.partial(panel_kernel, shards, blocks, parts, wanted)
    flops = 6 * len(wanted) * rows * shards * depth * width // 2
    before = [earlier[d] for d in wanted] if earlier else []
    found = call(kernel, outs, scratch, flops, where, *panel, *given, *before)
    return dict(zip(wanted, found, strict=True))


def after(value, *earlier):
    return lax.optimization_barrier((value, *earlier))[0]


def whole(pieces):
    return {(*place, 0): piece for place, piece in pieces.items()}


def together(*values):
    return list(lax.optimization_barrier(values))


class Grid:
    def __init__(self, mesh):
        self.rows = mesh.shape["row"]
        self.cols = mesh.shape["col"]
        self.shards = self.cols // self.rows

    def move(self, value, target):
        pairs = []
        for r in range(self.rows):
            for a in range(self.rows):
                for b in range(self.shards):
                    to = target(r, a, b)
                    if to is not None:
                        pairs.append((
                            r * self.cols + a * self.shards + b,
                            to[0] * self.cols + to[1] * self.shards + to[2],
                        ))
        return lax.ppermute(value, ("row", "col"), pairs)

    def swap(self, value):
        return self.move(value, lambda r, a, b: (a, r, b))

    def row_bit(self, value, bit):
        return self.move(value, lambda r, a, b: (r ^ bit, a, b))

    def gather_b(self, value):
        return {(0, o): self.b_bit(value, o) if o else value for o in range(self.shards)}

    def b_bit(self, value, bit):
        return self.move(value, lambda r, a, b: (r, a, b ^ bit))

    def gather_row(self, pieces):
        found = dict(pieces)
        for k in range(2, self.rows, 2):
            held = []
            for (_, o), piece in pieces.items():
                found[k // 2, o] = self.row_bit(after(piece, *held), k)
                held = [found[k // 2, 0]]
        return found

    def send(self, blocks, two_way):
        total = blocks[0]
        got = []
        for d in reversed(range(1, self.rows)):
            got.append(self.move(
                blocks[d],
                lambda r, a, b: (r, a ^ d, b)
                if (r ^ a ^ d) % 2 == 0 and (two_way or (a ^ d) > a) else None,
            ))
        for block in got:
            total = total + block
        return total

    def merged_send(self, blocks, two_way):
        def target(d):
            def to(r, a, b):
                odd = (r ^ a) % 2
                plane = a ^ d ^ odd
                if not two_way and plane < a:
                    return None
                return (r, plane, b) if odd else (r ^ 1, plane, b)

            return to

        got = [self.move(blocks[d], target(d)) for d in reversed(range(2, self.rows, 2))]
        got.append(self.move(
            blocks[1],
            lambda r, a, b: (r, a ^ 1, b) if (r ^ a) % 2 == 1 and (two_way or (a ^ 1) > a) else None,
        ))
        return sum(got, blocks[0])

    def both(self, total):
        return total, self.row_bit(total, 1)

    def pair_send(self, blocks, last):
        sums = {d: blocks[d] for d in range(0, self.rows, 2)}
        for d in reversed(range(3, self.rows, 2)):
            sums[d - 1] = sums[d - 1] + self.move(blocks[d], lambda r, a, b: (r, a ^ 1, b))
        got = [self.move(after(blocks[1], *last), lambda r, a, b: (r, a ^ 1, b))]
        for d in reversed(range(2, self.rows, 2)):
            got.append(self.move(sums[d], lambda r, a, b: (r, a ^ d, b)))
        return [blocks[0], *got]


def solution(mesh):
    grid = Grid(mesh)
    rows, shards = grid.rows, grid.shards

    def body(inv_diag, coupling, top_rhs, panel, rhs):
        r = lax.axis_index("row")
        c = lax.axis_index("col")
        a, b = c // shards, c % shards
        where = jnp.stack([b ^ o for o in range(shards)] + [a ^ r, r % 2]).astype(jnp.int32)
        planes = [a ^ d for d in range(rows)]
        slots = [(j ^ r) // 2 * 2 + j % 2 for j in planes] + [b ^ o for o in range(shards)]
        slots = jnp.stack(slots).astype(jnp.int32)
        run = functools.partial(stage, rows, where)
        width = top_rhs.shape[2]

        record_one = grid.swap(top_rhs[0])
        inverse_one = grid.gather_b(inv_diag[0])
        far = {(k // 2, 0): grid.row_bit(inv_diag[0], k) for k in range(2, rows, 2)}
        early = [record_one, *inverse_one.values(), *far.values()]
        half = inv_diag.shape[1] // 2
        inverse_one = {(*place, 0): piece for place, piece in (inverse_one | far).items()}
        for k in range(2, rows, 2):
            for o in range(1, shards):
                one, two = together(inverse_one[0, o, 0][:half], inverse_one[k // 2, 0, 0][half:])
                early += [one, two]
                inverse_one[k // 2, o, 0] = grid.row_bit(one, k)
                inverse_one[k // 2, o, half] = grid.b_bit(two, o)
        held = after(coupling, *early)
        coupled = grid.gather_b(held)
        coupled |= {(k // 2, 0): grid.row_bit(held, k) for k in range(2, rows, 2)}
        record_two = grid.swap(after(top_rhs[1], *early))
        first_in = grid.both(record_one)
        _, blocks = run(inverse_one, *first_in, record=True)
        blocks = together(*blocks, record_two)[:rows]

        for k in range(2, rows, 2):
            for o in range(1, shards):
                coupled[k // 2, o] = grid.row_bit(after(coupled[0, o], coupled[k // 2, 0]), k)
        panel_one = grid.gather_b(after(panel[0], *inverse_one.values()))
        held = after(inv_diag[1], *coupled.values())
        sums = list(grid.both(grid.merged_send(blocks, False)))
        first, blocks = run(whole(coupled), *sums, record=False)
        inverse_two = grid.gather_row(grid.gather_b(held))
        panel_two = grid.gather_b(after(panel[1], *panel_one.values()))
        sums = list(grid.both(grid.send(blocks, True)))
        sums[0] = after(sums[0], *panel_one.values())
        firsts = [[grid.row_bit(first, k) if k else first] for k in range(0, rows, 2)]
        _, blocks = run(whole(inverse_two), *grid.both(record_two), *sums, record=True)
        earlier = panel_product(slots, list(panel_one.values()), firsts, {}, list(range(rows)))
        blocks[1] = after(blocks[1], *panel_two.values())
        total = grid.send(blocks, False)
        total = after(total, *earlier.values())
        mine = functools.partial(lax.dynamic_slice_in_dim, start_index=r % 2 * width, slice_size=width, axis=1)
        solved_one = grid.swap(after(mine(first), total))
        far = [after(grid.row_bit(total, k), solved_one) for k in range(2, rows, 2)]
        seconds = [list(grid.both(value)) for value in [total, *far]]
        solved_two = grid.swap(mine(seconds[0][0] + seconds[0][1]))
        sent = list(range(3, rows, 2))
        ready = panel_product(slots, list(panel_two.values()), seconds, earlier, sent)
        held = list(panel_two.values())
        held[0] = after(held[0], *ready.values())
        rest = [d for d in reversed(range(rows)) if d not in sent]
        blocks = ready | panel_product(slots, held, seconds, earlier, rest)
        arrived = grid.pair_send(blocks, [solved_two])
        return jnp.stack([solved_one, solved_two]), rhs - sum(arrived[1:], arrived[0])

    in_specs = (
        P(None, "row", "col"),
        P("row", "col"),
        P(None, "row", "col"),
        P(None, "row", "col"),
        P("row", "col"),
    )
    out_specs = (P(None, "row", "col"), P("row", "col"))
    return jax.shard_map(body, mesh=mesh, in_specs=in_specs, out_specs=out_specs, check_vma=False)
```

```python
import functools

import jax
import jax.numpy as jnp
from jax import lax
from jax.experimental import pallas as pl
from jax.experimental.pallas import tpu as pltpu
from jax.sharding import PartitionSpec as P

F32 = jnp.float32
BF16 = jnp.bfloat16
VMEM_LIMIT = 32 * 1024 * 1024
SMEM = pl.BlockSpec(memory_space=pltpu.SMEM)
HBM = pl.BlockSpec(memory_space=pltpu.HBM)


def split(value):
    high = value.astype(BF16)
    return high, (value - high.astype(F32)).astype(BF16)


def dot(left, right):
    return jnp.dot(left, right, preferred_element_type=F32)


def product(left, right):
    return dot(left[0], right[0]) + (dot(left[0], right[1]) + dot(left[1], right[0]))


def shape(dtype, *dims):
    return jax.ShapeDtypeStruct(dims, dtype)


def call(kernel, outs, scratch, flops, where, *operands):
    moved = sum(v.size * v.dtype.itemsize for v in (*operands, *outs))
    return pl.pallas_call(
        kernel,
        out_shape=outs,
        in_specs=[SMEM] + [HBM] * len(operands),
        out_specs=[HBM] * len(outs),
        scratch_shapes=scratch,
        compiler_params=pltpu.CompilerParams(vmem_limit_bytes=VMEM_LIMIT),
        cost_estimate=pl.CostEstimate(flops=flops, bytes_accessed=moved, transcendentals=0),
    )(where, *operands)


def start(source, target, sem):
    copy = pltpu.make_async_copy(source, target, sem)
    copy.start()
    return copy


def stage_kernel(places, shards, blocks, record, keep, where_ref, *refs):
    count = len(places)
    outs = blocks // 2 + 1
    pieces, given = refs[:count], refs[count:-outs - keep - 6]
    vector_out, out_refs = refs[-outs - 7], refs[-outs - 6:-6]
    matrix_ref, given_ref, vector_ref, product_ref, sems, given_sems = refs[-6:]
    arrivals = [start(ref, given_ref.at[i], given_sems.at[i]) for i, ref in enumerate(given)] if not record else []
    core = where_ref[shards + 1]
    if record:
        width = given[0].shape[1]
        for i, side in enumerate((core, 1 - core)):
            lanes = pl.ds(pl.multiple_of(side * width, width), width)
            arrivals.append(start(given[i], vector_ref.at[:, lanes], given_sems.at[i]))
        arrivals += [start(ref, given_ref.at[i], given_sems.at[2 + i]) for i, ref in enumerate(given[2:])]
    copies = []
    for i, (k, o, row) in enumerate(places):
        part = matrix_ref.at[k, o, pl.ds(row, pieces[i].shape[0])]
        copies.append(start(pieces[i], part, sems.at[i]))
    offset = where_ref[shards]
    odd = lax.rem(offset, 2) == 1
    product_ref[blocks // 2] = jnp.zeros_like(product_ref[blocks // 2])
    for copy in arrivals:
        copy.wait()
    if not record:
        vector_ref[...] = given_ref[0] + given_ref[1]
    elif len(given) > 2:
        vector_ref[...] = vector_ref[...] - (given_ref[0] + given_ref[1])
    leaving = [start(vector_ref, vector_out, given_sems.at[0])] if keep else []
    depth = vector_ref.shape[0] // shards
    parts = [
        split(vector_ref[pl.ds(pl.multiple_of(where_ref[o] * depth, depth), depth), :]) for o in range(shards)
    ]
    for copy in copies:
        copy.wait()
    for i in reversed(range(blocks // 2)):
        k = jnp.bitwise_xor(offset, 2 * i) // 2
        sums = [product(split(matrix_ref[k, o]), parts[o]) for o in range(shards)]
        product_ref[i] = sum(sums[1:], sums[0])
        leaving.append(start(product_ref.at[i], out_refs[1 + i], sems.at[1 + i]))
    leaving.append(start(product_ref.at[jnp.where(odd, blocks // 2, 0)], out_refs[0], sems.at[0]))
    for copy in leaving:
        copy.wait()


def stage(blocks, where, matrix, *given, record, keep=False):
    rows, depth = matrix[0, 0, 0].shape
    shards = 1 + max(o for _, o, _ in matrix)
    width = given[0].shape[1] * (2 if record else 1)
    outs = [shape(F32, shards * depth, width)] * keep + [shape(F32, rows, width)] * (blocks // 2 + 1)
    scratch = [
        pltpu.VMEM((blocks // 2, shards, rows, depth), F32),
        pltpu.VMEM((2, shards * depth, width), F32),
        pltpu.VMEM((shards * depth, width), F32),
        pltpu.VMEM((blocks // 2 + 1, rows, width), F32),
        pltpu.SemaphoreType.DMA((max(len(matrix), blocks),)),
        pltpu.SemaphoreType.DMA((4,)),
    ]
    kernel = functools.partial(stage_kernel, list(matrix), shards, blocks, record, keep)
    flops = 3 * blocks * rows * shards * depth * width
    found = list(call(kernel, outs, scratch, flops, where, *matrix.values(), *given))
    vector = found.pop(0) if keep else None
    return vector, [found[0]] + [found[1 + d // 2] for d in range(1, blocks)]


def panel_kernel(shards, blocks, parts, wanted, where_ref, *refs):
    panels, pairs = refs[:shards], refs[shards:shards + blocks // 2 * parts]
    earlier = refs[shards + len(pairs):-len(wanted) - 9]
    outs = refs[-len(wanted) - 9:-9]
    panel_ref, pair_ref, p_high, p_low, v_high, v_low, total_ref, sems, out_sems = refs[-9:]
    width, depth = total_ref.shape[2], panel_ref.shape[2]
    copies = [start(ref, pair_ref.at[i], sems.at[i]) for i, ref in enumerate(pairs)]
    copies += [start(ref, panel_ref.at[o], sems.at[len(pairs) + o]) for o, ref in enumerate(panels)]
    loads = [start(ref, total_ref.at[d], out_sems.at[d]) for d, ref in enumerate(earlier)]
    for copy in copies[:len(pairs)]:
        copy.wait()
    for k in range(blocks // 2):
        for o in range(shards):
            rows = pl.ds(pl.multiple_of(where_ref[blocks + o] * depth, depth), depth)
            value = pair_ref[k * parts, rows, :]
            for i in range(1, parts):
                value = value + pair_ref[k * parts + i, rows, :]
            high, low = split(value)
            for side in range(2):
                lanes = slice(side * width, (side + 1) * width)
                v_high[2 * k + side, o * depth:(o + 1) * depth, :] = high[:, lanes]
                v_low[2 * k + side, o * depth:(o + 1) * depth, :] = low[:, lanes]
    for o, copy in enumerate(copies[len(pairs):]):
        copy.wait()
        p_high[:, o * depth:(o + 1) * depth], p_low[:, o * depth:(o + 1) * depth] = split(panel_ref[o])
    leaving = []
    for i, d in enumerate(wanted):
        k = where_ref[d]
        high, low = v_high[k], v_low[k]
        both = dot(p_high[...], jnp.concatenate([high, low], 1))
        total = both[:, :width] + (both[:, width:] + dot(p_low[...], high))
        if earlier:
            loads[i].wait()
            total = total_ref[i] + total
        total_ref[i] = total
        leaving.append(start(total_ref.at[i], outs[i], out_sems.at[i]))
    for copy in leaving:
        copy.wait()


def panel_product(where, panel, pairs, earlier, wanted):
    shards, blocks, parts = len(panel), len(pairs) * 2, len(pairs[0])
    rows, depth = panel[0].shape
    width = pairs[0][0].shape[1]
    given = [part for pair in pairs for part in pair]
    outs = [shape(F32, rows, width // 2)] * len(wanted)
    scratch = [
        pltpu.VMEM((shards, rows, depth), F32),
        pltpu.VMEM((len(given), shards * depth, width), F32),
        pltpu.VMEM((rows, shards * depth), BF16),
        pltpu.VMEM((rows, shards * depth), BF16),
        pltpu.VMEM((blocks, shards * depth, width // 2), BF16),
        pltpu.VMEM((blocks, shards * depth, width // 2), BF16),
        pltpu.VMEM((len(wanted), rows, width // 2), F32),
        pltpu.SemaphoreType.DMA((len(given) + shards,)),
        pltpu.SemaphoreType.DMA((len(wanted),)),
    ]
    kernel = functools.partial(panel_kernel, shards, blocks, parts, wanted)
    flops = 9 * len(wanted) * rows * shards * depth * width
    before = [earlier[d] for d in wanted] if earlier else []
    found = call(kernel, outs, scratch, flops, where, *panel, *given, *before)
    return dict(zip(wanted, found, strict=True))


def after(value, *earlier):
    return lax.optimization_barrier((value, *earlier))[0]


def whole(pieces):
    return {(*place, 0): piece for place, piece in pieces.items()}


def together(*values):
    return list(lax.optimization_barrier(values))


class Grid:
    def __init__(self, mesh):
        self.rows = mesh.shape["row"]
        self.cols = mesh.shape["col"]
        self.shards = self.cols // self.rows

    def move(self, value, target):
        pairs = []
        for r in range(self.rows):
            for a in range(self.rows):
                for b in range(self.shards):
                    to = target(r, a, b)
                    if to is not None:
                        pairs.append((
                            r * self.cols + a * self.shards + b,
                            to[0] * self.cols + to[1] * self.shards + to[2],
                        ))
        return lax.ppermute(value, ("row", "col"), pairs)

    def swap(self, value):
        return self.move(value, lambda r, a, b: (a, r, b))

    def row_bit(self, value, bit):
        return self.move(value, lambda r, a, b: (r ^ bit, a, b))

    def gather_b(self, value):
        return {(0, o): self.b_bit(value, o) if o else value for o in range(self.shards)}

    def b_bit(self, value, bit):
        return self.move(value, lambda r, a, b: (r, a, b ^ bit))

    def gather_row(self, pieces):
        found = dict(pieces)
        for k in range(2, self.rows, 2):
            held = []
            for (_, o), piece in pieces.items():
                found[k // 2, o] = self.row_bit(after(piece, *held), k)
                held = [found[k // 2, 0]]
        return found

    def send(self, blocks, two_way):
        total = blocks[0]
        got = []
        for d in reversed(range(1, self.rows)):
            got.append(self.move(
                blocks[d],
                lambda r, a, b: (r, a ^ d, b)
                if (r ^ a ^ d) % 2 == 0 and (two_way or (a ^ d) > a) else None,
            ))
        for block in got:
            total = total + block
        return total

    def merged_send(self, blocks, two_way):
        def target(d):
            def to(r, a, b):
                odd = (r ^ a) % 2
                plane = a ^ d ^ odd
                if not two_way and plane < a:
                    return None
                return (r, plane, b) if odd else (r ^ 1, plane, b)

            return to

        got = [self.move(blocks[d], target(d)) for d in reversed(range(2, self.rows, 2))]
        got.append(self.move(
            blocks[1],
            lambda r, a, b: (r, a ^ 1, b) if (r ^ a) % 2 == 1 and (two_way or (a ^ 1) > a) else None,
        ))
        return sum(got, blocks[0])

    def both(self, total):
        return total, self.row_bit(total, 1)

    def pair_send(self, blocks, last):
        sums = {d: blocks[d] for d in range(0, self.rows, 2)}
        for d in reversed(range(3, self.rows, 2)):
            sums[d - 1] = sums[d - 1] + self.move(blocks[d], lambda r, a, b: (r, a ^ 1, b))
        got = [self.move(after(blocks[1], *last, *[sums[d] for d in sums if d]), lambda r, a, b: (r, a ^ 1, b))]
        for d in reversed(range(2, self.rows, 2)):
            got.append(self.move(sums[d], lambda r, a, b: (r, a ^ d, b)))
        return [blocks[0], *got]


def solution(mesh):
    grid = Grid(mesh)
    rows, shards = grid.rows, grid.shards

    def body(inv_diag, coupling, top_rhs, panel, rhs):
        r = lax.axis_index("row")
        c = lax.axis_index("col")
        a, b = c // shards, c % shards
        where = jnp.stack([b ^ o for o in range(shards)] + [a ^ r, r % 2]).astype(jnp.int32)
        planes = [a ^ d for d in range(rows)]
        slots = [(j ^ r) // 2 * 2 + j % 2 for j in planes] + [b ^ o for o in range(shards)]
        slots = jnp.stack(slots).astype(jnp.int32)
        run = functools.partial(stage, rows, where)
        width = top_rhs.shape[2]

        record_one = grid.swap(top_rhs[0])
        inverse_one = grid.gather_b(inv_diag[0])
        far = {(k // 2, 0): grid.row_bit(inv_diag[0], k) for k in range(2, rows, 2)}
        early = [record_one, *inverse_one.values(), *far.values()]
        half = inv_diag.shape[1] // 2
        inverse_one = {(*place, 0): piece for place, piece in (inverse_one | far).items()}
        for k in range(2, rows, 2):
            for o in range(1, shards):
                one, two = together(inverse_one[0, o, 0][:half], inverse_one[k // 2, 0, 0][half:])
                early += [one, two]
                inverse_one[k // 2, o, 0] = grid.row_bit(one, k)
                inverse_one[k // 2, o, half] = grid.b_bit(two, o)
        held = after(coupling, *early)
        coupled = grid.gather_b(held)
        coupled |= {(k // 2, 0): grid.row_bit(held, k) for k in range(2, rows, 2)}
        record_two = grid.swap(after(top_rhs[1], *early))
        first_in = grid.both(record_one)
        _, blocks = run(inverse_one, *first_in, record=True)
        blocks = together(*blocks, record_two)[:rows]

        for k in range(2, rows, 2):
            for o in range(1, shards):
                coupled[k // 2, o] = grid.row_bit(after(coupled[0, o], coupled[k // 2, 0]), k)
        panel_one = grid.gather_b(after(panel[0], *inverse_one.values()))
        held = after(inv_diag[1], *coupled.values())
        sums = list(grid.both(grid.merged_send(blocks, False)))
        first, blocks = run(whole(coupled), *sums, record=False, keep=True)
        inverse_two = grid.gather_row(grid.gather_b(held))
        panel_two = grid.gather_b(after(panel[1], *panel_one.values()))
        sums = list(grid.both(grid.send(blocks, True)))
        sums[0] = after(sums[0], *panel_one.values())
        firsts = [[grid.row_bit(first, k) if k else first] for k in range(0, rows, 2)]
        _, blocks = run(whole(inverse_two), *grid.both(record_two), *sums, record=True)
        earlier = panel_product(slots, list(panel_one.values()), firsts, {}, list(range(rows)))
        blocks[1] = after(blocks[1], *panel_two.values())
        total = grid.send(blocks, False)
        total = after(total, *earlier.values())
        mine = functools.partial(lax.dynamic_slice_in_dim, start_index=r % 2 * width, slice_size=width, axis=1)
        solved_one = grid.swap(after(mine(first), total))
        far = [after(grid.row_bit(total, k), solved_one) for k in range(2, rows, 2)]
        seconds = [list(grid.both(value)) for value in [total, *far]]
        solved_two = grid.swap(mine(seconds[0][0] + seconds[0][1]))
        sent = list(range(3, rows, 2))
        ready = panel_product(slots, list(panel_two.values()), seconds, earlier, sent)
        held = list(panel_two.values())
        held[0] = after(held[0], *ready.values())
        rest = [d for d in reversed(range(rows)) if d not in sent]
        blocks = ready | panel_product(slots, held, seconds, earlier, rest)
        arrived = grid.pair_send(blocks, [solved_two])
        return jnp.stack([solved_one, solved_two]), rhs - sum(arrived[1:], arrived[0])

    in_specs = (
        P(None, "row", "col"),
        P("row", "col"),
        P(None, "row", "col"),
        P(None, "row", "col"),
        P("row", "col"),
    )
    out_specs = (P(None, "row", "col"), P("row", "col"))
    return jax.shard_map(body, mesh=mesh, in_specs=in_specs, out_specs=out_specs, check_vma=False)
```

```python
import functools

import jax
import jax.numpy as jnp
from jax import lax
from jax.experimental import pallas as pl
from jax.experimental.pallas import tpu as pltpu
from jax.sharding import PartitionSpec as P

F32 = jnp.float32
BF16 = jnp.bfloat16
VMEM_LIMIT = 32 * 1024 * 1024
SMEM = pl.BlockSpec(memory_space=pltpu.SMEM)
HBM = pl.BlockSpec(memory_space=pltpu.HBM)


def split(value):
    high = value.astype(BF16)
    return high, (value - high.astype(F32)).astype(BF16)


def dot(left, right):
    return jnp.dot(left, right, preferred_element_type=F32)


def product(left, right):
    return dot(left[0], right[0]) + (dot(left[0], right[1]) + dot(left[1], right[0]))


def shape(dtype, *dims):
    return jax.ShapeDtypeStruct(dims, dtype)


def call(kernel, outs, scratch, flops, where, *operands):
    moved = sum(v.size * v.dtype.itemsize for v in (*operands, *outs))
    return pl.pallas_call(
        kernel,
        out_shape=outs,
        in_specs=[SMEM] + [HBM] * len(operands),
        out_specs=[HBM] * len(outs),
        scratch_shapes=scratch,
        compiler_params=pltpu.CompilerParams(vmem_limit_bytes=VMEM_LIMIT),
        cost_estimate=pl.CostEstimate(flops=flops, bytes_accessed=moved, transcendentals=0),
    )(where, *operands)


def start(source, target, sem):
    copy = pltpu.make_async_copy(source, target, sem)
    copy.start()
    return copy


def stage_kernel(places, shards, blocks, record, keep, where_ref, *refs):
    count = len(places)
    outs = blocks // 2 + 1
    pieces, given = refs[:count], refs[count:-outs - keep - 6]
    vector_out, out_refs = refs[-outs - 7], refs[-outs - 6:-6]
    matrix_ref, given_ref, vector_ref, product_ref, sems, given_sems = refs[-6:]
    arrivals = [start(ref, given_ref.at[i], given_sems.at[i]) for i, ref in enumerate(given)] if not record else []
    core = where_ref[shards + 1]
    if record:
        width = given[0].shape[1]
        for i, side in enumerate((core, 1 - core)):
            lanes = pl.ds(pl.multiple_of(side * width, width), width)
            arrivals.append(start(given[i], vector_ref.at[:, lanes], given_sems.at[i]))
        arrivals += [start(ref, given_ref.at[i], given_sems.at[2 + i]) for i, ref in enumerate(given[2:])]
    copies = []
    for i, (k, o, row) in enumerate(places):
        part = matrix_ref.at[k, o, pl.ds(row, pieces[i].shape[0])]
        copies.append(start(pieces[i], part, sems.at[i]))
    offset = where_ref[shards]
    odd = lax.rem(offset, 2) == 1
    product_ref[blocks // 2] = jnp.zeros_like(product_ref[blocks // 2])
    for copy in arrivals:
        copy.wait()
    if not record:
        vector_ref[...] = given_ref[0] + given_ref[1]
    elif len(given) > 2:
        vector_ref[...] = vector_ref[...] - (given_ref[0] + given_ref[1])
    leaving = [start(vector_ref, vector_out, given_sems.at[0])] if keep else []
    depth = vector_ref.shape[0] // shards
    parts = [
        split(vector_ref[pl.ds(pl.multiple_of(where_ref[o] * depth, depth), depth), :]) for o in range(shards)
    ]
    for copy in copies:
        copy.wait()
    for i in reversed(range(blocks // 2)):
        k = jnp.bitwise_xor(offset, 2 * i) // 2
        sums = [product(split(matrix_ref[k, o]), parts[o]) for o in range(shards)]
        product_ref[i] = sum(sums[1:], sums[0])
        leaving.append(start(product_ref.at[i], out_refs[1 + i], sems.at[1 + i]))
    leaving.append(start(product_ref.at[jnp.where(odd, blocks // 2, 0)], out_refs[0], sems.at[0]))
    for copy in leaving:
        copy.wait()


def stage(blocks, where, matrix, *given, record, keep=False):
    depth = matrix[0, 0, 0].shape[1]
    rows = sum(piece.shape[0] for (k, o, _), piece in matrix.items() if k == o == 0)
    shards = 1 + max(o for _, o, _ in matrix)
    width = given[0].shape[1] * (2 if record else 1)
    outs = [shape(F32, shards * depth, width)] * keep + [shape(F32, rows, width)] * (blocks // 2 + 1)
    scratch = [
        pltpu.VMEM((blocks // 2, shards, rows, depth), F32),
        pltpu.VMEM((2, shards * depth, width), F32),
        pltpu.VMEM((shards * depth, width), F32),
        pltpu.VMEM((blocks // 2 + 1, rows, width), F32),
        pltpu.SemaphoreType.DMA((max(len(matrix), blocks),)),
        pltpu.SemaphoreType.DMA((4,)),
    ]
    kernel = functools.partial(stage_kernel, list(matrix), shards, blocks, record, keep)
    flops = 3 * blocks * rows * shards * depth * width
    found = list(call(kernel, outs, scratch, flops, where, *matrix.values(), *given))
    vector = found.pop(0) if keep else None
    return vector, [found[0]] + [found[1 + d // 2] for d in range(1, blocks)]


def panel_kernel(shards, blocks, parts, wanted, where_ref, *refs):
    panels, pairs = refs[:shards], refs[shards:shards + blocks // 2 * parts]
    earlier = refs[shards + len(pairs):-len(wanted) - 9]
    outs = refs[-len(wanted) - 9:-9]
    panel_ref, pair_ref, p_high, p_low, v_high, v_low, total_ref, sems, out_sems = refs[-9:]
    width, depth = total_ref.shape[2], panel_ref.shape[2]
    copies = [start(ref, pair_ref.at[i], sems.at[i]) for i, ref in enumerate(pairs)]
    copies += [start(ref, panel_ref.at[o], sems.at[len(pairs) + o]) for o, ref in enumerate(panels)]
    loads = [start(ref, total_ref.at[d], out_sems.at[d]) for d, ref in enumerate(earlier)]
    for copy in copies[:len(pairs)]:
        copy.wait()
    for k in range(blocks // 2):
        for o in range(shards):
            rows = pl.ds(pl.multiple_of(where_ref[blocks + o] * depth, depth), depth)
            value = pair_ref[k * parts, rows, :]
            for i in range(1, parts):
                value = value + pair_ref[k * parts + i, rows, :]
            high, low = split(value)
            for side in range(2):
                lanes = slice(side * width, (side + 1) * width)
                v_high[2 * k + side, o * depth:(o + 1) * depth, :] = high[:, lanes]
                v_low[2 * k + side, o * depth:(o + 1) * depth, :] = low[:, lanes]
    for o, copy in enumerate(copies[len(pairs):]):
        copy.wait()
        p_high[:, o * depth:(o + 1) * depth], p_low[:, o * depth:(o + 1) * depth] = split(panel_ref[o])
    leaving = []
    for i, d in enumerate(wanted):
        k = where_ref[d]
        high, low = v_high[k], v_low[k]
        both = dot(p_high[...], jnp.concatenate([high, low], 1))
        total = both[:, :width] + (both[:, width:] + dot(p_low[...], high))
        if earlier:
            loads[i].wait()
            total = total_ref[i] + total
        total_ref[i] = total
        leaving.append(start(total_ref.at[i], outs[i], out_sems.at[i]))
    for copy in leaving:
        copy.wait()


def panel_product(where, panel, pairs, earlier, wanted):
    shards, blocks, parts = len(panel), len(pairs) * 2, len(pairs[0])
    rows, depth = panel[0].shape
    width = pairs[0][0].shape[1]
    given = [part for pair in pairs for part in pair]
    outs = [shape(F32, rows, width // 2)] * len(wanted)
    scratch = [
        pltpu.VMEM((shards, rows, depth), F32),
        pltpu.VMEM((len(given), shards * depth, width), F32),
        pltpu.VMEM((rows, shards * depth), BF16),
        pltpu.VMEM((rows, shards * depth), BF16),
        pltpu.VMEM((blocks, shards * depth, width // 2), BF16),
        pltpu.VMEM((blocks, shards * depth, width // 2), BF16),
        pltpu.VMEM((len(wanted), rows, width // 2), F32),
        pltpu.SemaphoreType.DMA((len(given) + shards,)),
        pltpu.SemaphoreType.DMA((len(wanted),)),
    ]
    kernel = functools.partial(panel_kernel, shards, blocks, parts, wanted)
    flops = 9 * len(wanted) * rows * shards * depth * width
    before = [earlier[d] for d in wanted] if earlier else []
    found = call(kernel, outs, scratch, flops, where, *panel, *given, *before)
    return dict(zip(wanted, found, strict=True))


def after(value, *earlier):
    return lax.optimization_barrier((value, *earlier))[0]


def whole(pieces):
    return {(*place, 0): piece for place, piece in pieces.items()}


def together(*values):
    return list(lax.optimization_barrier(values))


class Grid:
    def __init__(self, mesh):
        self.rows = mesh.shape["row"]
        self.cols = mesh.shape["col"]
        self.shards = self.cols // self.rows

    def move(self, value, target):
        pairs = []
        for r in range(self.rows):
            for a in range(self.rows):
                for b in range(self.shards):
                    to = target(r, a, b)
                    if to is not None:
                        pairs.append((
                            r * self.cols + a * self.shards + b,
                            to[0] * self.cols + to[1] * self.shards + to[2],
                        ))
        return lax.ppermute(value, ("row", "col"), pairs)

    def swap(self, value):
        return self.move(value, lambda r, a, b: (a, r, b))

    def row_bit(self, value, bit):
        return self.move(value, lambda r, a, b: (r ^ bit, a, b))

    def gather_b(self, value):
        return {(0, o): self.b_bit(value, o) if o else value for o in range(self.shards)}

    def b_bit(self, value, bit):
        return self.move(value, lambda r, a, b: (r, a, b ^ bit))

    def gather_row(self, pieces):
        found = dict(pieces)
        for k in range(2, self.rows, 2):
            held = []
            for (_, o), piece in pieces.items():
                found[k // 2, o] = self.row_bit(after(piece, *held), k)
                held = [found[k // 2, 0]]
        return found

    def send(self, blocks, two_way):
        total = blocks[0]
        got = []
        for d in reversed(range(1, self.rows)):
            got.append(self.move(
                blocks[d],
                lambda r, a, b: (r, a ^ d, b)
                if (r ^ a ^ d) % 2 == 0 and (two_way or (a ^ d) > a) else None,
            ))
        for block in got:
            total = total + block
        return total

    def merged_send(self, blocks, two_way):
        def target(d):
            def to(r, a, b):
                odd = (r ^ a) % 2
                plane = a ^ d ^ odd
                if not two_way and plane < a:
                    return None
                return (r, plane, b) if odd else (r ^ 1, plane, b)

            return to

        got = [self.move(blocks[d], target(d)) for d in reversed(range(2, self.rows, 2))]
        got.append(self.move(
            blocks[1],
            lambda r, a, b: (r, a ^ 1, b) if (r ^ a) % 2 == 1 and (two_way or (a ^ 1) > a) else None,
        ))
        return sum(got, blocks[0])

    def both(self, total):
        return total, self.row_bit(total, 1)

    def pair_send(self, blocks, last):
        sums = {d: blocks[d] for d in range(0, self.rows, 2)}
        for d in reversed(range(3, self.rows, 2)):
            sums[d - 1] = sums[d - 1] + self.move(blocks[d], lambda r, a, b: (r, a ^ 1, b))
        got = [self.move(after(blocks[1], *last, *[sums[d] for d in sums if d]), lambda r, a, b: (r, a ^ 1, b))]
        for d in reversed(range(2, self.rows, 2)):
            got.append(self.move(sums[d], lambda r, a, b: (r, a ^ d, b)))
        return [blocks[0], *got]


def solution(mesh):
    grid = Grid(mesh)
    rows, shards = grid.rows, grid.shards

    def body(inv_diag, coupling, top_rhs, panel, rhs):
        r = lax.axis_index("row")
        c = lax.axis_index("col")
        a, b = c // shards, c % shards
        where = jnp.stack([b ^ o for o in range(shards)] + [a ^ r, r % 2]).astype(jnp.int32)
        planes = [a ^ d for d in range(rows)]
        slots = [(j ^ r) // 2 * 2 + j % 2 for j in planes] + [b ^ o for o in range(shards)]
        slots = jnp.stack(slots).astype(jnp.int32)
        run = functools.partial(stage, rows, where)
        width = top_rhs.shape[2]

        record_one = grid.swap(top_rhs[0])
        half = inv_diag.shape[1] // 2
        top, bottom = inv_diag[0][:half], inv_diag[0][half:]
        inverse_one = {(0, 0, 0): top, (0, 0, half): bottom}
        for o in range(1, shards):
            inverse_one[0, o, 0] = grid.b_bit(top, o)
        for k in range(2, rows, 2):
            inverse_one[k // 2, 0, half] = grid.row_bit(bottom, k)
        early = [record_one, *inverse_one.values()]
        for k in range(2, rows, 2):
            for o in range(1, shards):
                inverse_one[k // 2, o, 0] = grid.row_bit(inverse_one[0, o, 0], k)
                inverse_one[k // 2, o, half] = grid.b_bit(inverse_one[k // 2, 0, half], o)
        for o in range(1, shards):
            inverse_one[0, o, half] = grid.b_bit(bottom, o)
        for k in range(2, rows, 2):
            inverse_one[k // 2, 0, 0] = grid.row_bit(top, k)
        held = after(coupling, *early)
        coupled = grid.gather_b(held)
        coupled |= {(k // 2, 0): grid.row_bit(held, k) for k in range(2, rows, 2)}
        record_two = grid.swap(after(top_rhs[1], *early))
        first_in = grid.both(record_one)
        _, blocks = run(inverse_one, *first_in, record=True)
        blocks = together(*blocks, record_two)[:rows]

        for k in range(2, rows, 2):
            for o in range(1, shards):
                coupled[k // 2, o] = grid.row_bit(after(coupled[0, o], coupled[k // 2, 0]), k)
        panel_one = grid.gather_b(after(panel[0], *inverse_one.values()))
        held = after(inv_diag[1], *coupled.values())
        sums = list(grid.both(grid.merged_send(blocks, False)))
        first, blocks = run(whole(coupled), *sums, record=False, keep=True)
        inverse_two = grid.gather_row(grid.gather_b(held))
        panel_two = grid.gather_b(after(panel[1], *panel_one.values()))
        sums = list(grid.both(grid.send(blocks, True)))
        sums[0] = after(sums[0], *panel_one.values())
        firsts = [[grid.row_bit(first, k) if k else first] for k in range(0, rows, 2)]
        _, blocks = run(whole(inverse_two), *grid.both(record_two), *sums, record=True)
        earlier = panel_product(slots, list(panel_one.values()), firsts, {}, list(range(rows)))
        blocks[1] = after(blocks[1], *panel_two.values())
        total = grid.send(blocks, False)
        total = after(total, *earlier.values())
        mine = functools.partial(lax.dynamic_slice_in_dim, start_index=r % 2 * width, slice_size=width, axis=1)
        solved_one = grid.swap(after(mine(first), total))
        far = [after(grid.row_bit(total, k), solved_one) for k in range(2, rows, 2)]
        seconds = [list(grid.both(value)) for value in [total, *far]]
        solved_two = grid.swap(mine(seconds[0][0] + seconds[0][1]))
        sent = list(range(3, rows, 2))
        ready = panel_product(slots, list(panel_two.values()), seconds, earlier, sent)
        held = list(panel_two.values())
        held[0] = after(held[0], *ready.values())
        rest = [d for d in reversed(range(rows)) if d not in sent]
        blocks = ready | panel_product(slots, held, seconds, earlier, rest)
        arrived = grid.pair_send(blocks, [solved_two])
        return jnp.stack([solved_one, solved_two]), rhs - sum(arrived[1:], arrived[0])

    in_specs = (
        P(None, "row", "col"),
        P("row", "col"),
        P(None, "row", "col"),
        P(None, "row", "col"),
        P("row", "col"),
    )
    out_specs = (P(None, "row", "col"), P("row", "col"))
    return jax.shard_map(body, mesh=mesh, in_specs=in_specs, out_specs=out_specs, check_vma=False)
```

```python
import functools

import jax
import jax.numpy as jnp
from jax import lax
from jax.experimental import pallas as pl
from jax.experimental.pallas import tpu as pltpu
from jax.sharding import PartitionSpec as P

F32 = jnp.float32
BF16 = jnp.bfloat16
VMEM_LIMIT = 32 * 1024 * 1024
SMEM = pl.BlockSpec(memory_space=pltpu.SMEM)
HBM = pl.BlockSpec(memory_space=pltpu.HBM)


def split(value):
    high = value.astype(BF16)
    return high, (value - high.astype(F32)).astype(BF16)


def dot(left, right):
    return jnp.dot(left, right, preferred_element_type=F32)


def product(left, right):
    return dot(left[0], right[0]) + (dot(left[0], right[1]) + dot(left[1], right[0]))


def shape(dtype, *dims):
    return jax.ShapeDtypeStruct(dims, dtype)


def call(kernel, outs, scratch, flops, where, *operands):
    moved = sum(v.size * v.dtype.itemsize for v in (*operands, *outs))
    return pl.pallas_call(
        kernel,
        out_shape=outs,
        in_specs=[SMEM] + [HBM] * len(operands),
        out_specs=[HBM] * len(outs),
        scratch_shapes=scratch,
        compiler_params=pltpu.CompilerParams(vmem_limit_bytes=VMEM_LIMIT),
        cost_estimate=pl.CostEstimate(flops=flops, bytes_accessed=moved, transcendentals=0),
    )(where, *operands)


def start(source, target, sem):
    copy = pltpu.make_async_copy(source, target, sem)
    copy.start()
    return copy


def stage_kernel(places, shards, blocks, record, keep, where_ref, *refs):
    count = len(places)
    outs = blocks // 2 + 1
    pieces, given = refs[:count], refs[count:-outs - keep - 6]
    vector_out, out_refs = refs[-outs - 7], refs[-outs - 6:-6]
    matrix_ref, given_ref, vector_ref, product_ref, sems, given_sems = refs[-6:]
    arrivals = [start(ref, given_ref.at[i], given_sems.at[i]) for i, ref in enumerate(given)] if not record else []
    core = where_ref[shards + 1]
    if record:
        width = given[0].shape[1]
        for i, side in enumerate((core, 1 - core)):
            lanes = pl.ds(pl.multiple_of(side * width, width), width)
            arrivals.append(start(given[i], vector_ref.at[:, lanes], given_sems.at[i]))
        arrivals += [start(ref, given_ref.at[i], given_sems.at[2 + i]) for i, ref in enumerate(given[2:])]
    copies = []
    for i, (k, o, row) in enumerate(places):
        part = matrix_ref.at[k, o, pl.ds(row, pieces[i].shape[0])]
        copies.append(start(pieces[i], part, sems.at[i]))
    offset = where_ref[shards]
    odd = lax.rem(offset, 2) == 1
    product_ref[blocks // 2] = jnp.zeros_like(product_ref[blocks // 2])
    for copy in arrivals:
        copy.wait()
    if not record:
        vector_ref[...] = given_ref[0] + given_ref[1]
    elif len(given) > 2:
        vector_ref[...] = vector_ref[...] - (given_ref[0] + given_ref[1])
    leaving = [start(vector_ref, vector_out, given_sems.at[0])] if keep else []
    depth = vector_ref.shape[0] // shards
    parts = [
        split(vector_ref[pl.ds(pl.multiple_of(where_ref[o] * depth, depth), depth), :]) for o in range(shards)
    ]
    for copy in copies:
        copy.wait()
    for i in reversed(range(blocks // 2)):
        k = jnp.bitwise_xor(offset, 2 * i) // 2
        sums = [product(split(matrix_ref[k, o]), parts[o]) for o in range(shards)]
        product_ref[i] = sum(sums[1:], sums[0])
        leaving.append(start(product_ref.at[i], out_refs[1 + i], sems.at[1 + i]))
    leaving.append(start(product_ref.at[jnp.where(odd, blocks // 2, 0)], out_refs[0], sems.at[0]))
    for copy in leaving:
        copy.wait()


def stage(blocks, where, matrix, *given, record, keep=False):
    depth = matrix[0, 0, 0].shape[1]
    rows = sum(piece.shape[0] for (k, o, _), piece in matrix.items() if k == o == 0)
    shards = 1 + max(o for _, o, _ in matrix)
    width = given[0].shape[1] * (2 if record else 1)
    outs = [shape(F32, shards * depth, width)] * keep + [shape(F32, rows, width)] * (blocks // 2 + 1)
    scratch = [
        pltpu.VMEM((blocks // 2, shards, rows, depth), F32),
        pltpu.VMEM((2, shards * depth, width), F32),
        pltpu.VMEM((shards * depth, width), F32),
        pltpu.VMEM((blocks // 2 + 1, rows, width), F32),
        pltpu.SemaphoreType.DMA((max(len(matrix), blocks),)),
        pltpu.SemaphoreType.DMA((4,)),
    ]
    kernel = functools.partial(stage_kernel, list(matrix), shards, blocks, record, keep)
    flops = 3 * blocks * rows * shards * depth * width
    found = list(call(kernel, outs, scratch, flops, where, *matrix.values(), *given))
    vector = found.pop(0) if keep else None
    return vector, [found[0]] + [found[1 + d // 2] for d in range(1, blocks)]


def panel_kernel(shards, blocks, parts, wanted, where_ref, *refs):
    panels, pairs = refs[:shards], refs[shards:shards + blocks // 2 * parts]
    earlier = refs[shards + len(pairs):-len(wanted) - 9]
    outs = refs[-len(wanted) - 9:-9]
    panel_ref, pair_ref, p_high, p_low, v_high, v_low, total_ref, sems, out_sems = refs[-9:]
    width, depth = total_ref.shape[2], panel_ref.shape[2]
    copies = [start(ref, pair_ref.at[i], sems.at[i]) for i, ref in enumerate(pairs)]
    copies += [start(ref, panel_ref.at[o], sems.at[len(pairs) + o]) for o, ref in enumerate(panels)]
    loads = [start(ref, total_ref.at[d], out_sems.at[d]) for d, ref in enumerate(earlier)]
    for copy in copies[:len(pairs)]:
        copy.wait()
    for k in range(blocks // 2):
        for o in range(shards):
            rows = pl.ds(pl.multiple_of(where_ref[blocks + o] * depth, depth), depth)
            value = pair_ref[k * parts, rows, :]
            for i in range(1, parts):
                value = value + pair_ref[k * parts + i, rows, :]
            high, low = split(value)
            for side in range(2):
                lanes = slice(side * width, (side + 1) * width)
                v_high[2 * k + side, o * depth:(o + 1) * depth, :] = high[:, lanes]
                v_low[2 * k + side, o * depth:(o + 1) * depth, :] = low[:, lanes]
    for o, copy in enumerate(copies[len(pairs):]):
        copy.wait()
        p_high[:, o * depth:(o + 1) * depth], p_low[:, o * depth:(o + 1) * depth] = split(panel_ref[o])
    leaving = []
    for i, d in enumerate(wanted):
        k = where_ref[d]
        high, low = v_high[k], v_low[k]
        both = dot(p_high[...], jnp.concatenate([high, low], 1))
        total = both[:, :width] + (both[:, width:] + dot(p_low[...], high))
        if earlier:
            loads[i].wait()
            total = total_ref[i] + total
        total_ref[i] = total
        leaving.append(start(total_ref.at[i], outs[i], out_sems.at[i]))
    for copy in leaving:
        copy.wait()


def panel_product(where, panel, pairs, earlier, wanted):
    shards, blocks, parts = len(panel), len(pairs) * 2, len(pairs[0])
    rows, depth = panel[0].shape
    width = pairs[0][0].shape[1]
    given = [part for pair in pairs for part in pair]
    outs = [shape(F32, rows, width // 2)] * len(wanted)
    scratch = [
        pltpu.VMEM((shards, rows, depth), F32),
        pltpu.VMEM((len(given), shards * depth, width), F32),
        pltpu.VMEM((rows, shards * depth), BF16),
        pltpu.VMEM((rows, shards * depth), BF16),
        pltpu.VMEM((blocks, shards * depth, width // 2), BF16),
        pltpu.VMEM((blocks, shards * depth, width // 2), BF16),
        pltpu.VMEM((len(wanted), rows, width // 2), F32),
        pltpu.SemaphoreType.DMA((len(given) + shards,)),
        pltpu.SemaphoreType.DMA((len(wanted),)),
    ]
    kernel = functools.partial(panel_kernel, shards, blocks, parts, wanted)
    flops = 9 * len(wanted) * rows * shards * depth * width
    before = [earlier[d] for d in wanted] if earlier else []
    found = call(kernel, outs, scratch, flops, where, *panel, *given, *before)
    return dict(zip(wanted, found, strict=True))


def after(value, *earlier):
    return lax.optimization_barrier((value, *earlier))[0]


def whole(pieces):
    return {(*place, 0): piece for place, piece in pieces.items()}


def together(*values):
    return list(lax.optimization_barrier(values))


class Grid:
    def __init__(self, mesh):
        self.rows = mesh.shape["row"]
        self.cols = mesh.shape["col"]
        self.shards = self.cols // self.rows

    def move(self, value, target):
        pairs = []
        for r in range(self.rows):
            for a in range(self.rows):
                for b in range(self.shards):
                    to = target(r, a, b)
                    if to is not None:
                        pairs.append((
                            r * self.cols + a * self.shards + b,
                            to[0] * self.cols + to[1] * self.shards + to[2],
                        ))
        return lax.ppermute(value, ("row", "col"), pairs)

    def swap(self, value):
        return self.move(value, lambda r, a, b: (a, r, b))

    def row_bit(self, value, bit):
        return self.move(value, lambda r, a, b: (r ^ bit, a, b))

    def gather_b(self, value):
        return {(0, o): self.b_bit(value, o) if o else value for o in range(self.shards)}

    def b_bit(self, value, bit):
        return self.move(value, lambda r, a, b: (r, a, b ^ bit))

    def gather_row(self, pieces):
        found = dict(pieces)
        for k in range(2, self.rows, 2):
            held = []
            for (_, o), piece in pieces.items():
                found[k // 2, o] = self.row_bit(after(piece, *held), k)
                held = [found[k // 2, 0]]
        return found

    def send(self, blocks, two_way):
        total = blocks[0]
        got = []
        for d in reversed(range(1, self.rows)):
            got.append(self.move(
                blocks[d],
                lambda r, a, b: (r, a ^ d, b)
                if (r ^ a ^ d) % 2 == 0 and (two_way or (a ^ d) > a) else None,
            ))
        for block in got:
            total = total + block
        return total

    def merged_send(self, blocks, two_way):
        def target(d):
            def to(r, a, b):
                odd = (r ^ a) % 2
                plane = a ^ d ^ odd
                if not two_way and plane < a:
                    return None
                return (r, plane, b) if odd else (r ^ 1, plane, b)

            return to

        got = [self.move(blocks[d], target(d)) for d in reversed(range(2, self.rows, 2))]
        got.append(self.move(
            blocks[1],
            lambda r, a, b: (r, a ^ 1, b) if (r ^ a) % 2 == 1 and (two_way or (a ^ 1) > a) else None,
        ))
        return sum(got, blocks[0])

    def both(self, total):
        return total, self.row_bit(total, 1)

    def pair_send(self, blocks, last):
        sums = {d: blocks[d] for d in range(0, self.rows, 2)}
        for d in reversed(range(3, self.rows, 2)):
            sums[d - 1] = sums[d - 1] + self.move(blocks[d], lambda r, a, b: (r, a ^ 1, b))
        got = [self.move(after(blocks[1], *last, *[sums[d] for d in sums if d]), lambda r, a, b: (r, a ^ 1, b))]
        for d in reversed(range(2, self.rows, 2)):
            got.append(self.move(sums[d], lambda r, a, b: (r, a ^ d, b)))
        return [blocks[0], *got]


def solution(mesh):
    grid = Grid(mesh)
    rows, shards = grid.rows, grid.shards

    def body(inv_diag, coupling, top_rhs, panel, rhs):
        r = lax.axis_index("row")
        c = lax.axis_index("col")
        a, b = c // shards, c % shards
        where = jnp.stack([b ^ o for o in range(shards)] + [a ^ r, r % 2]).astype(jnp.int32)
        planes = [a ^ d for d in range(rows)]
        slots = [(j ^ r) // 2 * 2 + j % 2 for j in planes] + [b ^ o for o in range(shards)]
        slots = jnp.stack(slots).astype(jnp.int32)
        run = functools.partial(stage, rows, where)
        width = top_rhs.shape[2]

        record_one = grid.swap(top_rhs[0])
        half = inv_diag.shape[1] // 2
        top, bottom = inv_diag[0][:half], inv_diag[0][half:]
        inverse_one = {(0, 0, 0): top, (0, 0, half): bottom}
        for o in range(1, shards):
            inverse_one[0, o, 0] = grid.b_bit(top, o)
        for k in range(2, rows, 2):
            inverse_one[k // 2, 0, half] = grid.row_bit(bottom, k)
        early = [record_one, *inverse_one.values()]
        for k in range(2, rows, 2):
            for o in range(1, shards):
                inverse_one[k // 2, o, 0] = grid.row_bit(inverse_one[0, o, 0], k)
                inverse_one[k // 2, o, half] = grid.b_bit(inverse_one[k // 2, 0, half], o)
        for o in range(1, shards):
            inverse_one[0, o, half] = grid.b_bit(bottom, o)
        for k in range(2, rows, 2):
            inverse_one[k // 2, 0, 0] = grid.row_bit(top, k)
        held = after(coupling, *early)
        coupled = grid.gather_b(held)
        coupled |= {(k // 2, 0): grid.row_bit(held, k) for k in range(2, rows, 2)}
        record_two = grid.swap(after(top_rhs[1], record_one))
        first_in = grid.both(record_one)
        _, blocks = run(inverse_one, *first_in, record=True)
        blocks = together(*blocks, record_two)[:rows]

        for k in range(2, rows, 2):
            for o in range(1, shards):
                coupled[k // 2, o] = grid.row_bit(after(coupled[0, o], coupled[k // 2, 0]), k)
        panel_one = grid.gather_b(after(panel[0], *inverse_one.values()))
        held = after(inv_diag[1], *coupled.values())
        sums = list(grid.both(grid.merged_send(blocks, False)))
        first, blocks = run(whole(coupled), *sums, record=False, keep=True)
        inverse_two = grid.gather_row(grid.gather_b(held))
        panel_two = grid.gather_b(after(panel[1], *panel_one.values()))
        sums = list(grid.both(grid.send(blocks, True)))
        sums[0] = after(sums[0], *panel_one.values())
        firsts = [[grid.row_bit(first, k) if k else first] for k in range(0, rows, 2)]
        _, blocks = run(whole(inverse_two), *grid.both(record_two), *sums, record=True)
        earlier = panel_product(slots, list(panel_one.values()), firsts, {}, list(range(rows)))
        blocks[1] = after(blocks[1], *panel_two.values())
        total = grid.send(blocks, False)
        total = after(total, *earlier.values())
        mine = functools.partial(lax.dynamic_slice_in_dim, start_index=r % 2 * width, slice_size=width, axis=1)
        solved_one = grid.swap(mine(first))
        far = [after(grid.row_bit(total, k), solved_one) for k in range(2, rows, 2)]
        seconds = [list(grid.both(value)) for value in [total, *far]]
        solved_two = grid.swap(mine(seconds[0][0] + seconds[0][1]))
        sent = list(range(3, rows, 2))
        ready = panel_product(slots, list(panel_two.values()), seconds, earlier, sent)
        held = list(panel_two.values())
        held[0] = after(held[0], *ready.values())
        rest = [d for d in reversed(range(rows)) if d not in sent]
        blocks = ready | panel_product(slots, held, seconds, earlier, rest)
        arrived = grid.pair_send(blocks, [solved_two])
        return jnp.stack([solved_one, solved_two]), rhs - sum(arrived[1:], arrived[0])

    in_specs = (
        P(None, "row", "col"),
        P("row", "col"),
        P(None, "row", "col"),
        P(None, "row", "col"),
        P("row", "col"),
    )
    out_specs = (P(None, "row", "col"), P("row", "col"))
    return jax.shard_map(body, mesh=mesh, in_specs=in_specs, out_specs=out_specs, check_vma=False)
```
